32 devices in a mesh: width: 4 (over z), cb: 4 (over y, x), row: 2 (over core).
Axes of the slice: x: 2, y: 2, z: 4, core: 2. Of those that a mesh axis runs over, the one named last changes fastest.
Arguments:
- weights: bfloat16 [3584, 8192], P(('cb', 'row'), 'width'), as said below
- dir_codes: int32 [3584, 1024], P(('cb', 'row'), 'width'), may hold values from 0 to 65535
- norm_bins: int32 [3584, 1024], P(('cb', 'row'), 'width'), may hold values from 0 to 255, as said below
Outputs:
- codewords: float32 [4096, 128], P('cb')
- norm_levels: float32 [256], replicated
The draws below stay inside these ranges and needn't reach their ends.
Inputs may be any that keep to these rules, and one draw needn't show every extreme that they name: `weights`: real-valued entries, rows of differing scales. `norm_bins`: the bins of one row all lie in one aligned run of 16 consecutive bins.
All inputs are finite; a program needn't handle non-finite values.
Results may differ from the reference program's by a relative error of at most 0.0003.
Values sent between devices are 32-bit elements; how exact they have to be, the bound alone decides.
A program may use at most 192 MiB of HBM per device.

```python
import math
import jax
import jax.numpy as jnp
import numpy as np
from jax import lax

WIDTH = 8192
CODES = 65536
NBINS = 256
ROWS = 3584
GROUPS = 1024


def row_levels(key):
    base_levels = jnp.arange(ROWS, dtype=jnp.int32) % 16
    return jax.random.permutation(jax.random.fold_in(key, 11), base_levels)


def draw_weights(key, part):
    levels = row_levels(key)
    position = jnp.arange(ROWS, dtype=jnp.float32) / ROWS
    entries = jnp.clip(jax.random.normal(jax.random.fold_in(key, 12), (ROWS, WIDTH), jnp.float32), -6.0, 6.0)
    row_ramp = 1.0 + 2.0 * position
    scales = jnp.power(jnp.float32(1.25), levels.astype(jnp.float32)) * row_ramp
    return (entries * scales[:, None]).astype(jnp.bfloat16)


def draw_norm_bins(key, part):
    levels = row_levels(key)
    run_width = NBINS // 16
    offsets = jax.random.randint(jax.random.fold_in(key, 14), (ROWS, GROUPS), 0, run_width, dtype=jnp.int32)
    return levels[:, None] * run_width + offsets


def touch_ends(drawn, own_key, least, top_value):
    place = [jax.random.randint(jax.random.fold_in(own_key, axis), (), 0, length) for axis, length in enumerate(drawn.shape)]
    widest = drawn.shape.index(max(drawn.shape))
    next_to = place[:widest] + [(place[widest] + 1) % drawn.shape[widest]] + place[widest + 1:]
    return drawn.at[tuple(place)].set(least).at[tuple(next_to)].set(top_value)


def rank_bounds(count, slope):
    portions = [(1 << 20) // math.isqrt(grade ** slope) + 1 for grade in range(1, count + 1)]
    deviation = 1 + sum(portions) // (1 << 30)
    return np.cumsum(np.array([max(1, weight // deviation) for weight in portions]))


def ranked(own_key, extent, number_of, skew):
    listing = rank_bounds(number_of, skew)
    pick = jax.random.randint(jax.random.fold_in(own_key, 1), extent, 0, int(listing[number_of - 1]))
    standing = jnp.searchsorted(jnp.asarray(listing, jnp.int32), pick, side="right")
    return jax.random.permutation(jax.random.fold_in(own_key, 2), number_of)[standing].astype(jnp.int32)


def setup_inputs(seed: int = 0) -> dict:
    splits = jax.random.split(jax.random.key(seed), 4)
    return {
        "weights": draw_weights(jax.random.fold_in(splits[3], 71), 0),
        "dir_codes": touch_ends(ranked(splits[1], (ROWS, GROUPS), CODES, 3), jax.random.fold_in(splits[1], 3), 0, CODES - 1).astype(jnp.int32),
        "norm_bins": draw_norm_bins(jax.random.fold_in(splits[3], 71), 0),
    }


def hadamard_rows(row_data):
    row_count, width_now = row_data.shape
    half_span = 1
    while half_span < width_now:
        paired = row_data.reshape(row_count, width_now // (2 * half_span), 2, half_span)
        first = paired[:, :, 0]
        second = paired[:, :, 1]
        row_data = jnp.stack([first + second, first - second], axis=2).reshape(row_count, width_now)
        half_span = half_span * 2
    return row_data

def reference(weights, dir_codes, norm_bins):
    rotated = hadamard_rows(weights.astype(jnp.float32)) * (1.0 / math.sqrt(WIDTH))
    grouped = rotated.reshape(-1, 8)
    group_norms = jnp.sqrt(lax.optimization_barrier(jnp.sum(grouped * grouped, axis=-1)))
    floored = jnp.maximum(group_norms, 1.0)
    directions = grouped / floored[:, None]
    code_sums = jax.ops.segment_sum(directions, dir_codes.reshape(-1), num_segments=CODES)
    lengths = jnp.sqrt(lax.optimization_barrier(jnp.sum(code_sums * code_sums, axis=-1)))
    codewords = (code_sums / jnp.maximum(lengths, 1.0)[:, None]).reshape(CODES // 16, 128)
    log_norms = jnp.log(floored)
    bin_ids = norm_bins.reshape(-1)
    bin_sums = jax.ops.segment_sum(log_norms, bin_ids, num_segments=NBINS)
    bin_counts = jax.ops.segment_sum(jnp.ones_like(log_norms), bin_ids, num_segments=NBINS)
    norm_levels = bin_sums / jnp.maximum(bin_counts, 1.0)
    return (codewords, norm_levels)
```

```python
import functools
import math

import jax
import jax.numpy as jnp
from jax import lax
from jax.experimental import pallas as pl
from jax.experimental.pallas import tpu as pltpu
from jax.sharding import PartitionSpec as P

CODES = 65536
NBINS = 256
VECTOR = 8
RUN = 16
LANES = 256


def parity_sign(x):
    return 1 - 2 * (lax.population_count(x) & 1)


def rotate_kernel(rows, w_ref, y_ref):
    k = pl.program_id(0)
    cols = w_ref.shape[1]
    groups = cols // VECTOR
    i = lax.broadcasted_iota(jnp.int32, (cols, groups), 0)
    j = lax.broadcasted_iota(jnp.int32, (cols, groups), 1) * VECTOR + k
    h = parity_sign(i & j).astype(jnp.float32).astype(jnp.bfloat16)
    out = jnp.dot(w_ref[...], h, preferred_element_type=jnp.float32)
    parts, _, padded, _ = y_ref.shape
    for p in range(parts):
        y_ref[p, 0, :rows, :] = out[p * rows : (p + 1) * rows]
        if padded > rows:
            y_ref[p, 0, rows:, :] = jnp.zeros((padded - rows, groups), jnp.float32)


def rotate(weights, parts):
    total, cols = weights.shape
    rows = total // parts
    padded = -(-rows // 8) * 8
    groups = cols // VECTOR
    return pl.pallas_call(
        functools.partial(rotate_kernel, rows),
        grid=(VECTOR,),
        in_specs=[pl.BlockSpec((total, cols), lambda k: (0, 0))],
        out_specs=pl.BlockSpec((parts, 1, padded, groups), lambda k: (0, k, 0, 0)),
        out_shape=jax.ShapeDtypeStruct((parts, VECTOR, padded, groups), jnp.float32),
        compiler_params=pltpu.CompilerParams(vmem_limit_bytes=48 << 20),
        cost_estimate=pl.CostEstimate(
            flops=2 * total * cols * cols, bytes_accessed=total * cols * 6, transcendentals=0
        ),
        name="rotate",
    )(weights)


def table_kernel(parts, rows, owners, scale, pre_ref, post_ref, *refs):
    y_refs, code_refs, bin_refs = refs[:parts], refs[parts : 2 * parts], refs[2 * parts : 3 * parts]
    table_ref, bins_ref, d_ref, c_ref = refs[3 * parts :]
    step = pl.program_id(0)
    groups = y_refs[0].shape[2]

    @pl.when(step == 0)
    def _():
        table_ref[...] = jnp.zeros_like(table_ref)
        bins_ref[...] = jnp.zeros_like(bins_ref)

    row_ids = lax.broadcasted_iota(jnp.int32, (8, groups), 0) + step * 8
    square = [jnp.zeros((8, groups), jnp.float32) for _ in range(parts)]
    for k in range(VECTOR):
        z = [y_refs[p][k] * pre_ref[p] for p in range(parts)]
        half = 1
        while half < parts:
            z = [z[p ^ half] - z[p] if p & half else z[p] + z[p ^ half] for p in range(parts)]
            half *= 2
        for p in range(parts):
            value = z[p] * (post_ref[p] * scale)
            square[p] = square[p] + value * value
            d_ref[p, k] = value
    run_ids = lax.broadcasted_iota(jnp.int32, (8, NBINS), 1)
    sum_part = jnp.zeros((8, NBINS), jnp.float32)
    count_part = jnp.zeros((8, NBINS), jnp.float32)
    run = bin_refs[0][:, :1] // RUN
    logs, offsets, ones = [], [], []
    for p in range(parts):
        floored = jnp.maximum(jnp.sqrt(square[p]), 1.0)
        inverse = 1.0 / floored
        for k in range(VECTOR):
            d_ref[p, k] = d_ref[p, k] * inverse
        c_ref[p] = code_refs[p][...]
        logs.append(jnp.log(floored))
        offsets.append(bin_refs[p][...] % RUN)
        ones.append((row_ids < rows).astype(jnp.float32))
    for b in range(RUN):
        s = sum(jnp.where(offsets[p] == b, logs[p], 0.0) for p in range(parts))
        n = sum(jnp.where(offsets[p] == b, ones[p], 0.0) for p in range(parts))
        here = run_ids == run * RUN + b
        sum_part = sum_part + jnp.where(here, jnp.sum(s, axis=1, keepdims=True), 0.0)
        count_part = count_part + jnp.where(here, jnp.sum(n, axis=1, keepdims=True), 0.0)
    bins_ref[0] += sum_part
    bins_ref[1] += count_part

    low = CODES // LANES // owners

    def body(index, _):
        p, r = index // 8, index % 8
        code = c_ref[p, pl.ds(r, 1), :]
        u, v = code // LANES, code % LANES
        sub = lax.broadcasted_iota(jnp.int32, (LANES, groups), 0)
        hot_u = (sub == u).astype(jnp.float32).astype(jnp.bfloat16)
        hot_v = (sub == v).astype(jnp.float32).astype(jnp.bfloat16)
        hot_v = jnp.concatenate([hot_v, hot_v], axis=1)
        spread = []
        for k in range(VECTOR):
            d = jnp.broadcast_to(d_ref[p, k, pl.ds(r, 1), :], (16, groups))
            top = d.astype(jnp.bfloat16)
            rest = (d - top.astype(jnp.float32)).astype(jnp.bfloat16)
            spread.append((top, rest))
        blocks = []
        for o in range(owners):
            for k in range(VECTOR):
                for t in range(low // 16):
                    hot = hot_u[o * low + t * 16 : o * low + t * 16 + 16]
                    blocks.append(jnp.concatenate([hot * spread[k][0], hot * spread[k][1]], axis=1))
        left = jnp.concatenate(blocks, axis=0)
        table_ref[...] += lax.dot_general(
            left, hot_v, (((1,), (1,)), ((), ())), preferred_element_type=jnp.float32
        )
        return 0

    lax.fori_loop(0, parts * 8, body, 0)


def table(ys, codes, bins, pre, post, rows, owners):
    parts = len(ys)
    _, padded, groups = ys[0].shape
    scale = 1.0 / math.sqrt(groups * VECTOR * parts)
    height = VECTOR * CODES // LANES
    smem = pl.BlockSpec(memory_space=pltpu.SMEM)
    return pl.pallas_call(
        functools.partial(table_kernel, parts, rows, owners, scale),
        grid=(padded // 8,),
        in_specs=[smem, smem]
        + [pl.BlockSpec((VECTOR, 8, groups), lambda i: (0, i, 0))] * parts
        + [pl.BlockSpec((8, groups), lambda i: (i, 0))] * (2 * parts),
        out_specs=[
            pl.BlockSpec((height, LANES), lambda i: (0, 0)),
            pl.BlockSpec((2, 8, NBINS), lambda i: (0, 0, 0)),
        ],
        out_shape=[
            jax.ShapeDtypeStruct((height, LANES), jnp.float32),
            jax.ShapeDtypeStruct((2, 8, NBINS), jnp.float32),
        ],
        scratch_shapes=[
            pltpu.VMEM((parts, VECTOR, 8, groups), jnp.float32),
            pltpu.VMEM((parts, 8, groups), jnp.int32),
        ],
        compiler_params=pltpu.CompilerParams(vmem_limit_bytes=48 << 20),
        cost_estimate=pl.CostEstimate(
            flops=4 * parts * padded * groups * CODES * VECTOR,
            bytes_accessed=parts * padded * groups * 40,
            transcendentals=0,
        ),
        name="direction_table",
    )(pre, post, *ys, *codes, *bins)


def exchanged(array, axis, parts, me):
    def block(d):
        return lax.dynamic_index_in_dim(array, me ^ d, 0, keepdims=False)

    return [block(0)] + [
        lax.ppermute(block(d), axis, [(i, i ^ d) for i in range(parts)]) for d in range(1, parts)
    ]


def per_device(weights, dir_codes, norm_bins):
    parts, owners = lax.axis_size("width"), lax.axis_size("cb")
    me = lax.axis_index("width")
    rows = weights.shape[0] // parts
    padded = -(-rows // 8) * 8

    def split(ids):
        ids = ids.reshape(parts, rows, -1)
        return jnp.pad(ids, ((0, 0), (0, padded - rows), (0, 0)))

    codes = exchanged(split(dir_codes), "width", parts, me)
    bins = exchanged(split(norm_bins), "width", parts, me)
    ys = exchanged(rotate(weights, parts), "width", parts, me)
    others = jnp.arange(parts, dtype=jnp.int32)
    pre = parity_sign(others & me).astype(jnp.float32)
    post = parity_sign((others ^ me) & me).astype(jnp.float32)
    sums, bin_part = table(ys, codes, bins, pre, post, rows, owners)
    bin_part = lax.psum(jnp.sum(bin_part, axis=1), ("width", "cb", "row"))
    norm_levels = bin_part[0] / jnp.maximum(bin_part[1], 1.0)
    owned = lax.psum_scatter(sums.reshape(-1, 128), "cb", scatter_dimension=0, tiled=True)
    owned = lax.psum(owned, ("width", "row")).reshape(VECTOR, -1)
    lengths = jnp.sqrt(jnp.sum(owned * owned, axis=0))
    words = owned / jnp.maximum(lengths, 1.0)[None]
    return (words.T.reshape(-1, 128), norm_levels)


def solution(mesh):
    spec = P(("cb", "row"), "width")
    return jax.shard_map(
        per_device,
        mesh=mesh,
        in_specs=(spec, spec, spec),
        out_specs=(P("cb", None), P()),
        check_vma=False,
    )
```

```python
import functools
import math

import jax
import jax.numpy as jnp
from jax import lax
from jax.experimental import pallas as pl
from jax.experimental.pallas import tpu as pltpu
from jax.sharding import PartitionSpec as P

CODES = 65536
NBINS = 256
VECTOR = 8
RUN = 16
LANES = 256
JOIN = 2


def parity_sign(x):
    return 1 - 2 * (lax.population_count(x) & 1)


def rotate_kernel(rows, w_ref, y_ref):
    k = pl.program_id(0)
    cols = w_ref.shape[1]
    groups = cols // VECTOR
    i = lax.broadcasted_iota(jnp.int32, (cols, groups), 0)
    j = lax.broadcasted_iota(jnp.int32, (cols, groups), 1) * VECTOR + k
    h = parity_sign(i & j).astype(jnp.float32).astype(jnp.bfloat16)
    out = jnp.dot(w_ref[...], h, preferred_element_type=jnp.float32)
    parts, _, padded, _ = y_ref.shape
    for p in range(parts):
        y_ref[p, 0, :rows, :] = out[p * rows : (p + 1) * rows]
        if padded > rows:
            y_ref[p, 0, rows:, :] = jnp.zeros((padded - rows, groups), jnp.float32)


def rotate(weights, parts):
    total, cols = weights.shape
    rows = total // parts
    padded = -(-rows // 8) * 8
    groups = cols // VECTOR
    return pl.pallas_call(
        functools.partial(rotate_kernel, rows),
        grid=(VECTOR,),
        in_specs=[pl.BlockSpec((total, cols), lambda k: (0, 0))],
        out_specs=pl.BlockSpec((parts, 1, padded, groups), lambda k: (0, k, 0, 0)),
        out_shape=jax.ShapeDtypeStruct((parts, VECTOR, padded, groups), jnp.float32),
        compiler_params=pltpu.CompilerParams(vmem_limit_bytes=48 << 20),
        cost_estimate=pl.CostEstimate(
            flops=2 * total * cols * cols, bytes_accessed=total * cols * 6, transcendentals=0
        ),
        name="rotate",
    )(weights)


def table_kernel(parts, rows, first, owners, scale, pre_ref, post_ref, *refs):
    y_refs, code_refs, bin_refs = refs[:parts], refs[parts : 2 * parts], refs[2 * parts : 3 * parts]
    *before, table_ref, bins_ref, d_ref, c_ref = refs[3 * parts :]
    step = pl.program_id(0)
    groups = y_refs[0].shape[2]

    @pl.when(step == 0)
    def _():
        table_ref[...] = before[0][...] if before else jnp.zeros_like(table_ref)
        bins_ref[...] = before[1][...] if before else jnp.zeros_like(bins_ref)

    row_ids = lax.broadcasted_iota(jnp.int32, (8, groups), 0) + (step * 8 + first)
    square = [jnp.zeros((8, groups), jnp.float32) for _ in range(parts)]
    for k in range(VECTOR):
        z = [y_refs[p][k] * pre_ref[p] for p in range(parts)]
        half = 1
        while half < parts:
            z = [z[p ^ half] - z[p] if p & half else z[p] + z[p ^ half] for p in range(parts)]
            half *= 2
        for p in range(parts):
            value = z[p] * (post_ref[p] * scale)
            square[p] = square[p] + value * value
            d_ref[p, k] = value
    run_ids = lax.broadcasted_iota(jnp.int32, (8, NBINS), 1)
    sum_part = jnp.zeros((8, NBINS), jnp.float32)
    count_part = jnp.zeros((8, NBINS), jnp.float32)
    run = bin_refs[0][:, :1] // RUN
    logs, offsets, ones = [], [], []
    for p in range(parts):
        floored = jnp.maximum(jnp.sqrt(square[p]), 1.0)
        inverse = 1.0 / floored
        for k in range(VECTOR):
            d_ref[p, k] = d_ref[p, k] * inverse
        c_ref[p] = code_refs[p][...]
        logs.append(jnp.log(floored))
        offsets.append(bin_refs[p][...] % RUN)
        ones.append((row_ids < rows).astype(jnp.float32))
    for b in range(RUN):
        s = sum(jnp.where(offsets[p] == b, logs[p], 0.0) for p in range(parts))
        n = sum(jnp.where(offsets[p] == b, ones[p], 0.0) for p in range(parts))
        here = run_ids == run * RUN + b
        sum_part = sum_part + jnp.where(here, jnp.sum(s, axis=1, keepdims=True), 0.0)
        count_part = count_part + jnp.where(here, jnp.sum(n, axis=1, keepdims=True), 0.0)
    bins_ref[0] += sum_part
    bins_ref[1] += count_part

    low = CODES // LANES // owners

    def body(index, _):
        p, r = index // 8 * JOIN, index % 8
        lefts, rights = [], []
        for q in range(JOIN):
            code = c_ref[p + q, pl.ds(r, 1), :]
            u, v = code // LANES, code % LANES
            sub = lax.broadcasted_iota(jnp.int32, (LANES, groups), 0)
            hot_u = (sub == u).astype(jnp.float32).astype(jnp.bfloat16)
            hot_v = (sub == v).astype(jnp.float32).astype(jnp.bfloat16)
            rights += [hot_v, hot_v]
            tops, rests = [], []
            spread = []
            for k in range(VECTOR):
                d = jnp.broadcast_to(d_ref[p + q, k, pl.ds(r, 1), :], (16, groups))
                top = d.astype(jnp.bfloat16)
                spread.append((top, (d - top.astype(jnp.float32)).astype(jnp.bfloat16)))
            for o in range(owners):
                for k in range(VECTOR):
                    for t in range(low // 16):
                        hot = hot_u[o * low + t * 16 : o * low + t * 16 + 16]
                        tops.append(hot * spread[k][0])
                        rests.append(hot * spread[k][1])
            lefts += [jnp.concatenate(tops, axis=0), jnp.concatenate(rests, axis=0)]
        table_ref[...] += lax.dot_general(
            jnp.concatenate(lefts, axis=1),
            jnp.concatenate(rights, axis=1),
            (((1,), (1,)), ((), ())),
            preferred_element_type=jnp.float32,
        )
        return 0

    lax.fori_loop(0, parts // JOIN * 8, body, 0)


def table(ys, codes, bins, pre, post, rows, first, owners, before):
    parts = len(ys)
    _, padded, groups = ys[0].shape
    scale = 1.0 / math.sqrt(groups * VECTOR * parts)
    height = VECTOR * CODES // LANES
    smem = pl.BlockSpec(memory_space=pltpu.SMEM)
    sums_spec = pl.BlockSpec((height, LANES), lambda i: (0, 0))
    bins_spec = pl.BlockSpec((2, 8, NBINS), lambda i: (0, 0, 0))
    return pl.pallas_call(
        functools.partial(table_kernel, parts, rows, first, owners, scale),
        grid=(padded // 8,),
        in_specs=[smem, smem]
        + [pl.BlockSpec((VECTOR, 8, groups), lambda i: (0, i, 0))] * parts
        + [pl.BlockSpec((8, groups), lambda i: (i, 0))] * (2 * parts)
        + [sums_spec, bins_spec][: len(before)],
        out_specs=[sums_spec, bins_spec],
        out_shape=[
            jax.ShapeDtypeStruct((height, LANES), jnp.float32),
            jax.ShapeDtypeStruct((2, 8, NBINS), jnp.float32),
        ],
        scratch_shapes=[
            pltpu.VMEM((parts, VECTOR, 8, groups), jnp.float32),
            pltpu.VMEM((parts, 8, groups), jnp.int32),
        ],
        compiler_params=pltpu.CompilerParams(vmem_limit_bytes=48 << 20),
        cost_estimate=pl.CostEstimate(
            flops=4 * parts * padded * groups * CODES * VECTOR,
            bytes_accessed=parts * padded * groups * 40,
            transcendentals=0,
        ),
        name="direction_table",
    )(pre, post, *ys, *codes, *bins, *before)


def reduce_kernel(phases, owners, low, t_ref, b_ref, words_ref, levels_ref, *scratch):
    count = len(phases)
    recvs, held = scratch[:count], scratch[count : 2 * count]
    bin_recv, bin_held, send, recv, bin_send, bin_got, gather_send, gather_got = scratch[2 * count :]
    places = {axis: lax.axis_index(axis) for axis, _ in phases}
    partners = [{axis: places[axis] ^ bit} for axis, bit in phases]
    barrier = pltpu.get_barrier_semaphore()
    for partner in partners:
        pl.semaphore_signal(barrier, inc=1, device_id=partner, device_id_type=pl.DeviceIdType.MESH)
    pl.semaphore_wait(barrier, count)

    bin_held[0] = jnp.sum(b_ref[...], axis=1)
    now, many, height, offset = t_ref, owners, low, 0
    gathers = []
    for n, (axis, bit) in enumerate(phases):
        mine = places[axis] // bit % 2
        if axis == "cb":
            many //= 2
            source = now.at[pl.ds((1 - mine) * many, many)]
            kept = now.at[pl.ds(mine * many, many)]
        elif height > 8:
            height //= 2
            source = now.at[:, :, pl.ds(pl.multiple_of((1 - mine) * height, 8), height)]
            kept = now.at[:, :, pl.ds(pl.multiple_of(mine * height, 8), height)]
            offset = offset + mine * height
            gathers.append((n, height, offset))
        else:
            source, kept = now, now
        main = pltpu.make_async_remote_copy(
            src_ref=source,
            dst_ref=recvs[n],
            send_sem=send.at[n],
            recv_sem=recv.at[n],
            device_id=partners[n],
            device_id_type=pl.DeviceIdType.MESH,
        )
        side = pltpu.make_async_remote_copy(
            src_ref=bin_held.at[n],
            dst_ref=bin_recv.at[n],
            send_sem=bin_send.at[n],
            recv_sem=bin_got.at[n],
            device_id=partners[n],
            device_id_type=pl.DeviceIdType.MESH,
        )
        main.start()
        side.start()
        side.wait()
        bin_held[n + 1] = bin_held[n] + bin_recv[n]
        main.wait()
        held[n][...] = kept[...] + recvs[n][...]
        now = held[n]

    totals = bin_held[count]
    levels_ref[...] = totals[:1] / jnp.maximum(totals[1:], 1.0)

    values = [now[0, k] for k in range(VECTOR)]
    lengths = jnp.sqrt(sum(value * value for value in values))
    inverse = 1.0 / jnp.maximum(lengths, 1.0)
    across = 128 // VECTOR
    down = LANES // across
    line = lax.broadcasted_iota(jnp.int32, (down, LANES), 0)
    spot = lax.broadcasted_iota(jnp.int32, (down, LANES), 1)
    chosen = spot // across == line
    source = lax.broadcasted_iota(jnp.int32, (LANES, 128), 0)
    target = lax.broadcasted_iota(jnp.int32, (LANES, 128), 1)
    total = jnp.zeros((height * down, 128), jnp.float32)
    for k in range(VECTOR):
        value = values[k] * inverse
        spread = jnp.concatenate(
            [
                jnp.where(chosen, jnp.broadcast_to(value[i : i + 1], (down, LANES)), 0.0)
                for i in range(height)
            ],
            axis=0,
        )
        select = (target == source % across * VECTOR + k).astype(jnp.float32).astype(jnp.bfloat16)
        for _ in range(3):
            part = spread.astype(jnp.bfloat16)
            total = total + jnp.dot(part, select, preferred_element_type=jnp.float32)
            spread = spread - part.astype(jnp.float32)
    words_ref[pl.ds(pl.multiple_of(offset * down, 8), height * down), :] = total

    for n, size, start in reversed(gathers):
        region = words_ref.at[pl.ds(pl.multiple_of(start * down, 8), size * down)]
        copy = pltpu.make_async_remote_copy(
            src_ref=region,
            dst_ref=region,
            send_sem=gather_send.at[n],
            recv_sem=gather_got.at[n],
            device_id=partners[n],
            device_id_type=pl.DeviceIdType.MESH,
        )
        copy.start()
        copy.wait()


def reduced(sums, bin_part, parts, owners, cores):
    low = CODES // LANES // owners

    def bits(axis, size):
        return [(axis, 1 << n) for n in range(size.bit_length() - 1)]

    phases = bits("row", cores) + bits("cb", owners)[::-1] + bits("width", parts)
    count = len(phases)
    buffers = []
    many, height = owners, low
    for axis, _ in phases:
        if axis == "cb":
            many //= 2
        elif height > 8:
            height //= 2
        buffers.append(pltpu.VMEM((many, VECTOR, height, LANES), jnp.float32))
    vmem = pl.BlockSpec(memory_space=pltpu.VMEM)
    dma = pltpu.SemaphoreType.DMA((count,))
    return pl.pallas_call(
        functools.partial(reduce_kernel, phases, owners, low),
        in_specs=[vmem, vmem],
        out_specs=[vmem, vmem],
        out_shape=[
            jax.ShapeDtypeStruct((CODES * VECTOR // owners // 128, 128), jnp.float32),
            jax.ShapeDtypeStruct((1, NBINS), jnp.float32),
        ],
        scratch_shapes=buffers
        + buffers
        + [
            pltpu.VMEM((count, 2, NBINS), jnp.float32),
            pltpu.VMEM((count + 1, 2, NBINS), jnp.float32),
        ]
        + [dma] * 6,
        compiler_params=pltpu.CompilerParams(
            collective_id=0, has_side_effects=True, vmem_limit_bytes=32 << 20
        ),
        name="reduce_words",
    )(sums.reshape(owners, VECTOR, low, LANES), bin_part)


def exchanged(array, axis, parts, me):
    def block(d):
        return lax.dynamic_index_in_dim(array, me ^ d, 0, keepdims=False)

    return [block(0)] + [
        lax.ppermute(block(d), axis, [(i, i ^ d) for i in range(parts)]) for d in range(1, parts)
    ]


def per_device(weights, dir_codes, norm_bins):
    parts, owners, cores = (lax.axis_size(axis) for axis in ("width", "cb", "row"))
    me = lax.axis_index("width")
    rows = weights.shape[0] // parts
    padded = -(-rows // 8) * 8

    def split(ids):
        ids = ids.reshape(parts, rows, -1)
        return jnp.pad(ids, ((0, 0), (0, padded - rows), (0, 0)))

    others = jnp.arange(parts, dtype=jnp.int32)
    pre = parity_sign(others & me).astype(jnp.float32)
    post = parity_sign((others ^ me) & me).astype(jnp.float32)
    codes, bins, turned = split(dir_codes), split(norm_bins), rotate(weights, parts)
    edge = max(padded // 8 // 4, 1) * 8
    chunks = [(0, edge), (edge, padded)]
    arrived = []
    for start, stop in chunks:
        sent = (turned[:, :, start:stop], codes[:, start:stop], bins[:, start:stop])
        if arrived:
            sent, arrived[-1] = lax.optimization_barrier((sent, arrived[-1]))
        arrived.append([exchanged(array, "width", parts, me) for array in sent])
    before = []
    for (start, _), (ys, ids, runs) in zip(chunks, arrived):
        before = table(ys, ids, runs, pre, post, rows, start, owners, before)
    codewords, norm_levels = reduced(*before, parts, owners, cores)
    return (codewords, norm_levels.reshape(-1))


def solution(mesh):
    spec = P(("cb", "row"), "width")
    return jax.shard_map(
        per_device,
        mesh=mesh,
        in_specs=(spec, spec, spec),
        out_specs=(P("cb", None), P()),
        check_vma=False,
    )
```
